512 devices in a mesh: ka: 8 (over x, core), pts: 64 (over z, y).
Axes of the slice: x: 4, y: 4, z: 16, core: 2. Of those that a mesh axis runs over, the one named last changes fastest.
Arguments:
- orbitals: bfloat16 [216, 2, 4096, 384], P('ka', None, 'pts'), may hold values from -1.5 to 1.5
- counts: int32 [216], P('ka'), may hold values from 60 to 300
- occupation: float32 [216, 384], P('ka'), may hold values from 0.2 to 1
- coulomb: bfloat16 [216, 2, 64, 4096], P('ka', None, None, 'pts'), may hold values from -24 to 24
Outputs:
- exchange_block: bfloat16 [216, 2, 64, 4096], P('ka', None, None, 'pts')
The draws below stay inside these ranges and needn't reach their ends.
Inputs may be any that keep to these rules, and one draw needn't show every extreme that they name: `counts`: between 60 and 300 occupied bands per k-point.
All inputs are finite; a program needn't handle non-finite values.
Results may differ from the reference program's by a relative error of at most 0.0057.
Values may be sent and summed in bfloat16 or wider, within the bound.
A program may use at most 64 MiB of HBM per device.

```python
import jax
import jax.numpy as jnp
from jax import lax

NMU = 4096
NB = 384
KSIDE = 6
ROW_DEV = 1
NK = 216
ROWS = 64
N_PTS = 64


def with_ends(drawn, own_key, smallest, top_value):
    shape = drawn.shape
    index_at = [jax.random.randint(jax.random.fold_in(own_key, axis), (), 0, shape[axis]) for axis in range(len(shape))]
    drawn = drawn.at[tuple(index_at)].set(smallest)
    longest = shape.index(max(shape))
    index_at[longest] = (index_at[longest] + 1) % shape[longest]
    return drawn.at[tuple(index_at)].set(top_value)


def block_scale(own_key, extent, shards, smallest, high):
    loudness, own = 1.0, jax.random.fold_in(own_key, 6)
    for position, blocks in shards:
        heights = jnp.exp(jax.random.uniform(jax.random.fold_in(own, position), (blocks,), jnp.float32, smallest / len(shards), high / len(shards)))
        loudness = loudness * jnp.repeat(heights, extent[position] // blocks).reshape([-1 if axis == position else 1 for axis in range(len(extent))])
    return loudness


def normal_values(key, extent, spread, most, cuts=(), kind=jnp.bfloat16):
    values = spread * jax.random.normal(key, extent, jnp.float32)
    if cuts:
        values = values * block_scale(key, extent, cuts, -0.22, 0.18)
    return jnp.clip(values, -most, most).astype(kind)


def setup_inputs(seed: int = 0) -> dict:
    streams_of = jax.random.split(jax.random.key(seed), 5)
    orbitals = normal_values(streams_of[0], (NK, 2, NMU, NB), 0.25, 1.5, ((0, 8), (2, 64)))
    counts = with_ends(jax.random.randint(streams_of[1], (NK,), 5 * NB // 32, 25 * NB // 32 + 1), jax.random.fold_in(streams_of[1], 1), 5 * NB // 32, (25 * NB // 32 + 1) - 1).astype(jnp.int32)
    occupation = jnp.clip(0.2 + 0.8 * jax.random.uniform(streams_of[2], (NK, NB), jnp.float32) ** block_scale(streams_of[2], (NK, NB), ((0, 8),), -0.2, 0.2), 0.2, 1.0)
    coulomb = normal_values(streams_of[3], (NK, 2, ROWS, NMU), 4.0, 24.0, ((0, 8), (3, 64)))
    return {"orbitals": orbitals, "counts": counts, "occupation": occupation, "coulomb": coulomb}


def slab_points():
    pts_dev = NMU // N_PTS
    rows = jnp.arange(ROWS, dtype=jnp.int32)
    return ((rows // ROW_DEV) * pts_dev + rows % ROW_DEV).astype(jnp.int32)


def reference(orbitals, counts, occupation, coulomb):
    band = jnp.arange(NB, dtype=jnp.int32)
    weights = jnp.where(band[None, :] < counts[:, None], occupation, jnp.float32(0.0)).astype(jnp.float32)
    slab = jnp.take(orbitals, slab_points(), axis=2).astype(jnp.float32)
    weighted = (slab * weights[:, None, None, :]).astype(jnp.bfloat16)
    weighted = lax.optimization_barrier(weighted).astype(jnp.float32)
    left_re = weighted[:, 0]
    left_im = weighted[:, 1]

    def one_block(start):
        cols = lax.dynamic_slice_in_dim(orbitals, start, 512, 2).astype(jnp.float32)
        right_re = cols[:, 0]
        right_im = cols[:, 1]
        real = jnp.einsum('krb,knb->krn', left_re, right_re) + jnp.einsum('krb,knb->krn', left_im, right_im)
        imag = jnp.einsum('krb,knb->krn', left_im, right_re) - jnp.einsum('krb,knb->krn', left_re, right_im)
        real = lax.optimization_barrier(real.astype(jnp.bfloat16)).astype(jnp.float32)
        imag = lax.optimization_barrier(imag.astype(jnp.bfloat16)).astype(jnp.float32)
        density = (real + 1j * imag).reshape(KSIDE, KSIDE, KSIDE, ROWS, 512)
        kernel = lax.dynamic_slice_in_dim(coulomb, start, 512, 3).astype(jnp.float32)
        kernel = (kernel[:, 0] + 1j * kernel[:, 1]).reshape(KSIDE, KSIDE, KSIDE, ROWS, 512)
        product = jnp.fft.fftn(kernel, axes=(0, 1, 2)) * jnp.fft.fftn(density, axes=(0, 1, 2))
        result = -jnp.fft.ifftn(product, axes=(0, 1, 2)) / NK
        result = result.reshape(NK, ROWS, 512)
        return jnp.stack([jnp.real(result), jnp.imag(result)], 1).astype(jnp.bfloat16)

    starts = (jnp.arange(NMU // 512, dtype=jnp.int32) * 512).astype(jnp.int32)
    blocks = lax.map(one_block, starts)
    blocks = jnp.moveaxis(blocks, 0, 3)
    return blocks.reshape(NK, 2, ROWS, NMU)
```

```python
import functools

import jax
import jax.numpy as jnp
import numpy as np
from jax import lax
from jax.experimental import pallas as pl
from jax.experimental.pallas import tpu as pltpu
from jax.sharding import Mesh
from jax.sharding import PartitionSpec as P

KSIDE = 6
PTS = ("pts_0", "pts_1")
KA = ("ka_0", "ka_1")
MESH = pl.DeviceIdType.MESH

NKD = 27
KP = 32
NA = 18
NB = NKD - NA
PLANES = 5
RA = 96
RB = 48
RD = RA + RB
LANES = 128
HALF = 64
ROOT = float(np.sqrt(3.0) / 2.0)


def transform_table():
    index = np.arange(KSIDE**3)
    xyz = np.stack([index // 36, index // 6 % 6, index % 6], 1)
    phase = (xyz @ xyz.T) % KSIDE
    cosine = np.array([1.0, 0.5, -0.5, -1.0, -0.5, 0.5])[phase]
    sine = np.array([0.0, 1.0, 1.0, 0.0, -1.0, -1.0])[phase]
    place = index // NKD * KP + index % NKD
    table = np.zeros((2, 8 * KP, 8 * KP), np.float32)
    table[0][np.ix_(place, place)] = cosine
    table[1][np.ix_(place, place)] = sine
    return table.reshape(2 * 8 * KP, 8 * KP)


def kernel(
    orb_hbm, counts_ref, occ_ref, cou_hbm, table_ref, out_ref,
    orb, cou, right, gath, spread, wide, dense, vsend, vrecv, vhat_a, vhat_b, dsend, drecv, osend, orecv,
    in_sem, s1, r1, s2, r2, s3a, r3a, s3b, r3b, sx, rx,
):
    z0, y0 = lax.axis_index("pts_0"), lax.axis_index("pts_1")
    a0 = lax.axis_index("ka_0") * 2 + lax.axis_index("ka_1")
    zq0, zr0 = z0 // 4, lax.rem(z0, 4)

    def zdev(d):
        return {"pts_0": lax.rem(z0 + d + 16, 16)}

    def ydev(d):
        return {"pts_1": lax.rem(y0 + d, 4)}

    def adev(d):
        a = lax.rem(a0 + d, 8)
        return {"ka_0": a // 2, "ka_1": lax.rem(a, 2)}

    load_orb = pltpu.make_async_copy(orb_hbm, orb, in_sem.at[0])
    load_cou = pltpu.make_async_copy(cou_hbm, cou, in_sem.at[1])
    load_orb.start()
    load_cou.start()

    barrier = pltpu.get_barrier_semaphore()
    peers = [zdev(d) for d in (8, 4, -4, 2, -2, 1, -1)] + [ydev(d) for d in (1, 2, 3)] + [adev(d) for d in range(1, 8)]
    for peer in peers:
        pl.semaphore_signal(barrier, inc=1, device_id=peer, device_id_type=MESH)

    lane = lax.broadcasted_iota(jnp.int32, (1, LANES), 1)
    low = lane < HALF
    plus = jnp.where(low, 1.0, -1.0).astype(jnp.float32)

    def swap(x):
        return pltpu.roll(x, HALF, 1)

    square = (NKD, NKD)
    on = lax.broadcasted_iota(jnp.int32, square, 0) == lax.broadcasted_iota(jnp.int32, square, 1)
    counts = jnp.sum(jnp.where(on, counts_ref[...].astype(jnp.float32), 0.0), axis=1, keepdims=True)
    band = lax.broadcasted_iota(jnp.int32, (NKD, 3 * LANES), 1).astype(jnp.float32)
    weights = jnp.where(band < counts, occ_ref[...], 0.0)

    load_orb.wait()
    for k in range(NKD):
        for c in range(2):
            wide[c * KP + k : c * KP + k + 1, :] = orb[k, c, 0:1, :].astype(jnp.float32) * weights[k : k + 1, :]
    parts = []
    for c in range(2):
        parts.append(wide[c * KP : c * KP + NKD, :])
    rest = jnp.where(low, parts[0][:, 256:], swap(parts[1][:, 256:]))
    planes = [parts[0][:, :128], parts[1][:, :128], parts[0][:, 128:256], parts[1][:, 128:256], rest]
    lead = jnp.concatenate([p[:NA] for p in planes] + [jnp.zeros((RA - PLANES * NA, LANES), jnp.float32)], 0)
    tail = jnp.concatenate([p[NA:] for p in planes] + [jnp.zeros((RB - PLANES * NB, LANES), jnp.float32)], 0)
    gath[zr0, zq0, y0, 0:RA, :] = lead.astype(jnp.bfloat16)
    gath[zr0, zq0, y0, RA:RD, :] = tail.astype(jnp.bfloat16)

    pl.semaphore_wait(barrier, len(peers))

    def send(src, dst, ssem, rsem, peer):
        return pltpu.make_async_remote_copy(
            src_ref=src, dst_ref=dst, send_sem=ssem, recv_sem=rsem, device_id=peer, device_id_type=MESH
        )

    sent = []

    def go(copy):
        copy.start()
        sent.append(copy)

    def first(i, zq):
        ref = gath.at[zr0, zq, y0]
        return send(ref, ref, s1.at[i], r1.at[i], zdev((4, -4, 8)[i]))

    def side(zr, y, rows, i, send_sem, recv_sem):
        part = (pl.ds(0, 4), pl.ds(0, 4), pl.ds(0, 2), pl.ds(2, 2))[i]
        ref = gath.at[zr, part, y, rows]
        return send(ref, ref, send_sem, recv_sem, zdev((1, -1, 2, -2)[i]))

    def across(zr, y, rows, j, send_sem, recv_sem):
        ref = gath.at[zr, :, y, rows]
        return send(ref, ref, send_sem, recv_sem, ydev((1, 3, 2)[j]))

    rows_a, rows_b = pl.ds(0, RA), pl.ds(RA, RB)
    from_z = (3, 1, 2, 2)
    from_y = (3, 1, 2)

    def res(d):
        return lax.rem(zr0 + d, 4)

    def yy(d):
        return lax.rem(y0 + d, 4)

    def scatter(zr, y, rows, base, zqs):
        def one(zq, carry):
            r = (zq * 4 + zr) * 4 + y
            block = gath[zr, zq, y, rows, :].astype(jnp.float32)
            spread[pl.ds(base * 64 + r, rows.size, stride=64), :] = block
            return carry

        lax.fori_loop(zqs[0], zqs[1], one, 0)

    def scatter_a(zr, y):
        scatter(zr, y, rows_a, 0, (0, 4))

    def scatter_b(zr, y, zqs=(0, 4)):
        scatter(zr, y, rows_b, RA, zqs)

    for i in (2, 0, 1):
        go(first(i, zq0))

    load_cou.wait()
    for k in range(NKD, KP):
        wide_rows = pl.ds(k, 64, stride=KP)
        vhat_a[wide_rows, :] = jnp.zeros((64, LANES), jnp.float32)

    def lay(k, carry):
        pair = jnp.concatenate([cou[k, 0], cou[k, 1]], axis=1).astype(jnp.float32)
        vhat_a[pl.ds(k, 64, stride=KP), :] = pair
        return carry

    lax.fori_loop(0, NKD, lay, 0)
    vsend[...] = vhat_a[...].astype(jnp.bfloat16).reshape(8, 8, KP, LANES)

    def swap_out(stage, src, dst_of, d):
        return send(src, dst_of, sx.at[stage, d - 1], rx.at[stage, d - 1], adev(d))

    def to_mine(stage, buffer, landing, d):
        return swap_out(stage, buffer.at[lax.rem(a0 + d, 8)], landing.at[:, a0], d)

    for d in range(1, 8):
        go(to_mine(0, vsend, vrecv, d))
    vrecv[:, a0] = vsend[a0]

    for i, d in ((0, -4), (1, 4), (2, 8)):
        first(i, lax.rem(zq0 + d // 4 + 4, 4)).wait_recv()
    for i in range(4):
        go(side(zr0, y0, rows_a, i, s2.at[i], r2.at[i]))
    for j in range(3):
        go(across(zr0, y0, rows_b, j, s2.at[4 + j], r2.at[4 + j]))
    for j in range(3):
        go(across(zr0, y0, rows_a, j, s3a.at[j, 0], r3a.at[j, 0]))
    for i in range(4):
        go(side(zr0, y0, rows_b, i, s3b.at[i, 0], r3b.at[i, 0]))
    scatter_a(zr0, y0)
    scatter_b(zr0, y0)

    def turn(k, carry):
        re, im = orb[k, 0], orb[k, 1]
        minus = -im
        rest_re = jnp.where(low, re[:, 256:].astype(jnp.float32), swap(im[:, 256:].astype(jnp.float32)))
        rest_im = jnp.where(low, minus[:, 256:].astype(jnp.float32), swap(re[:, 256:].astype(jnp.float32)))
        right[k, 0:64, :] = jnp.concatenate(
            [re[:, :128], im[:, :128], re[:, 128:256], im[:, 128:256], rest_re.astype(jnp.bfloat16)], 1
        )
        right[k, 64:128, :] = jnp.concatenate(
            [minus[:, :128], re[:, :128], minus[:, 128:256], re[:, 128:256], rest_im.astype(jnp.bfloat16)], 1
        )
        return carry

    lax.fori_loop(0, NKD, turn, 0)

    groups_z = (((0,), 1), ((1,), 2), ((2, 3), 3))
    for which, order in groups_z:
        for i in which:
            side(res(from_z[i]), y0, rows_a, i, s2.at[i], r2.at[i]).wait_recv()
        for j in range(3):
            go(across(res(from_z[which[0]]), y0, rows_a, j, s3a.at[j, order], r3a.at[j, order]))
        j = order - 1
        across(zr0, yy(from_y[j]), rows_b, j, s2.at[4 + j], r2.at[4 + j]).wait_recv()
        for i in range(4):
            go(side(zr0, yy(from_y[j]), rows_b, i, s3b.at[i, order], r3b.at[i, order]))
    for which, order in groups_z:
        scatter_a(res(from_z[which[0]]), y0)
        scatter_b(zr0, yy(from_y[order - 1]))

    deltas_z = (0,) + tuple(from_z[which[0]] for which, _ in groups_z)
    deltas_y = (0,) + from_y

    def forward(x):
        y = jnp.dot(table_ref[...], x, preferred_element_type=jnp.float32)
        return y[: 8 * KP] + (ROOT * plus) * swap(y[8 * KP :])

    for d in range(1, 8):
        to_mine_from = swap_out(0, vsend.at[0], vrecv.at[:, lax.rem(a0 + 8 - d, 8)], d)
        to_mine_from.wait_recv()

    def kern(r, carry):
        v = forward(vrecv[r].reshape(8 * KP, LANES))
        w = swap(v)
        rows = pl.ds(pl.multiple_of(r * 8 * KP, 8 * KP), 8 * KP)
        vhat_a[rows, :] = jnp.where(low, v, w)
        vhat_b[rows, :] = jnp.where(low, -w, v)
        return carry

    lax.fori_loop(0, 8, kern, 0)

    for order in range(4):
        for j in range(3):
            zr, y = res(deltas_z[order]), yy(from_y[j])
            across(zr, y, rows_a, j, s3a.at[j, order], r3a.at[j, order]).wait_recv()
            scatter_a(zr, y)
        for i in range(4):
            zr, y = res(from_z[i]), yy(deltas_y[order])
            side(zr, y, rows_b, i, s3b.at[i, order], r3b.at[i, order]).wait_recv()
            scatter_b(zr, y, ((0, 4), (0, 4), (0, 2), (2, 4))[i])

    for k in range(NKD, KP):
        dense[pl.ds(k, 64, stride=KP), :] = jnp.zeros((64, LANES), jnp.float32)

    def dens(base, count, start):
        def one(k, carry):
            left = [
                spread[pl.ds(pl.multiple_of((base + j * count + k) * 64, 64), 64), :].astype(jnp.bfloat16)
                for j in range(PLANES)
            ]
            d = lax.dot_general(
                jnp.concatenate(left, 1), right[start + k], (((1,), (1,)), ((), ())), preferred_element_type=jnp.float32
            )
            dense[pl.ds(start + k, 64, stride=KP), :] = d
            return carry

        lax.fori_loop(0, count, one, 0)

    dens(0, NA, 0)
    dens(RA, NB, NA)
    dsend[...] = dense[...].astype(jnp.bfloat16).reshape(8, 8, KP, LANES)
    for d in range(1, 8):
        go(to_mine(1, dsend, drecv, d))
    drecv[:, a0] = dsend[a0]
    for d in range(1, 8):
        swap_out(1, dsend.at[0], drecv.at[:, lax.rem(a0 + 8 - d, 8)], d).wait_recv()

    scale = -1.0 / float(KSIDE**6)

    def conv(r, carry):
        d = forward(drecv[r].reshape(8 * KP, LANES))
        rows = pl.ds(pl.multiple_of(r * 8 * KP, 8 * KP), 8 * KP)
        product = vhat_a[rows, :] * d + vhat_b[rows, :] * swap(d)
        y = jnp.dot(table_ref[...], product.astype(jnp.bfloat16), preferred_element_type=jnp.float32)
        back = scale * y[: 8 * KP] - (scale * ROOT * plus) * swap(y[8 * KP :])
        osend[r] = back.astype(jnp.bfloat16).reshape(8, KP, LANES)
        return carry

    lax.fori_loop(0, 8, conv, 0)

    def home(d):
        mine = pl.ds(pl.multiple_of(a0 * 8, 8), 8)
        return swap_out(2, osend.at[:, lax.rem(a0 + d, 8)], orecv.at[mine], d)

    for d in range(1, 8):
        go(home(d))
    orecv[pl.ds(pl.multiple_of(a0 * 8, 8), 8)] = osend[:, a0]
    for d in range(1, 8):
        theirs = pl.ds(pl.multiple_of(lax.rem(a0 + 8 - d, 8) * 8, 8), 8)
        swap_out(2, osend.at[:, 0], orecv.at[theirs], d).wait_recv()

    def unlay(r, carry):
        spread[pl.ds(r, KP, stride=64), :] = orecv[r].astype(jnp.float32)
        return carry

    lax.fori_loop(0, 64, unlay, 0)

    def finish(k, carry):
        o = spread[pl.ds(pl.multiple_of(k * 64, 64), 64), :]
        out_ref[k, 0] = o[:, :HALF].astype(jnp.bfloat16)
        out_ref[k, 1] = swap(o)[:, :HALF].astype(jnp.bfloat16)
        return carry

    lax.fori_loop(0, NKD, finish, 0)
    for copy in sent:
        copy.wait_send()


def local(orbitals, counts, occupation, coulomb):
    table = jnp.asarray(transform_table(), jnp.bfloat16)
    bf, f32 = jnp.bfloat16, jnp.float32
    vmem = pl.BlockSpec(memory_space=pltpu.VMEM)
    anywhere = pl.BlockSpec(memory_space=pl.ANY)
    dma = pltpu.SemaphoreType.DMA
    return pl.pallas_call(
        kernel,
        out_shape=jax.ShapeDtypeStruct((NKD, 2, 64, 64), bf),
        in_specs=[anywhere, vmem, vmem, anywhere, vmem],
        out_specs=vmem,
        scratch_shapes=[
            pltpu.VMEM((NKD, 2, 64, 384), bf),
            pltpu.VMEM((NKD, 2, 64, 64), bf),
            pltpu.VMEM((NKD, 128, PLANES * LANES), bf),
            pltpu.VMEM((4, 4, 4, RD, LANES), bf),
            pltpu.VMEM((RD * 64, LANES), f32),
            pltpu.VMEM((2 * KP, 384), f32),
            pltpu.VMEM((64 * KP, LANES), f32),
            pltpu.VMEM((8, 8, KP, LANES), bf),
            pltpu.VMEM((8, 8, KP, LANES), bf),
            pltpu.VMEM((64 * KP, LANES), f32),
            pltpu.VMEM((64 * KP, LANES), f32),
            pltpu.VMEM((8, 8, KP, LANES), bf),
            pltpu.VMEM((8, 8, KP, LANES), bf),
            pltpu.VMEM((8, 8, KP, LANES), bf),
            pltpu.VMEM((64, KP, LANES), bf),
            dma((2,)),
            dma((3,)),
            dma((3,)),
            dma((7,)),
            dma((7,)),
            dma((3, 4)),
            dma((3, 4)),
            dma((4, 4)),
            dma((4, 4)),
            dma((3, 7)),
            dma((3, 7)),
        ],
        compiler_params=pltpu.CompilerParams(
            collective_id=0, has_side_effects=True, vmem_limit_bytes=48 * 1024 * 1024
        ),
    )(orbitals, counts.reshape(1, NKD), occupation, coulomb, table)


def solution(mesh):
    finer = Mesh(mesh.devices.reshape(4, 2, 16, 4), ("ka_0", "ka_1", "pts_0", "pts_1"))
    in_specs = (P(KA, None, PTS, None), P(KA), P(KA, None), P(KA, None, None, PTS))
    out_specs = P(KA, None, None, PTS)
    return jax.shard_map(local, mesh=finer, in_specs=in_specs, out_specs=out_specs, check_vma=False)
```

```python
import functools

import jax
import jax.numpy as jnp
import numpy as np
from jax import lax
from jax.experimental import pallas as pl
from jax.experimental.pallas import tpu as pltpu
from jax.sharding import Mesh
from jax.sharding import PartitionSpec as P

KSIDE = 6
PTS = ("pts_0", "pts_1")
KA = ("ka_0", "ka_1")
MESH = pl.DeviceIdType.MESH

NKD = 27
KP = 32
PLANES = 5
RD = 144
LANES = 128
HALF = 64
PTILE = 8 * KP
ROOT = float(np.sqrt(3.0) / 2.0)
SCALE = -1.0 / float(KSIDE**6)

DELTA_Y = (0, 1, 3, 2)
STAGES = ((0, 1), (1, 2), (3, 1))
OFFSETS = (0, -1, 1, -2, 2, -4, 4, -5, 3, -3, 5, -6, 6, 8, 7, -7)
NEAR = {0: (1, -1, 2, -2), -4: (1, -1, 2), 4: (1, -1, -2), 8: (1, -1)}
CUT = 80


def transform_table():
    index = np.arange(KSIDE**3)
    xyz = np.stack([index // 36, index // 6 % 6, index % 6], 1)
    phase = (xyz @ xyz.T) % KSIDE
    cosine = np.array([1.0, 0.5, -0.5, -1.0, -0.5, 0.5])[phase]
    sine = np.array([0.0, 1.0, 1.0, 0.0, -1.0, -1.0])[phase]
    place = index // NKD * KP + index % NKD
    table = np.zeros((2, PTILE, PTILE), np.float32)
    table[0][np.ix_(place, place)] = cosine
    table[1][np.ix_(place, place)] = sine
    return table.reshape(2 * PTILE, PTILE)


def kernel(
    orb_hbm, counts_hbm, occ_hbm, cou_hbm, table_hbm, out_ref,
    row, counts_ref, occ_ref, orb, cou, table_ref,
    right, gath, spread, wide, dense, vsend, vrecv, vhat_a, vhat_b, dsend, drecv, osend, orecv,
    in_sem, sz, rz, sy, ry, sf, rf, sx, rx,
):
    z0, y0 = lax.axis_index("pts_0"), lax.axis_index("pts_1")
    a0 = lax.axis_index("ka_0") * 2 + lax.axis_index("ka_1")

    def zdev(d):
        return {"pts_0": lax.rem(z0 + d + 16, 16)}

    def ydev(d):
        return {"pts_1": lax.rem(y0 + d, 4)}

    def adev(d):
        a = lax.rem(a0 + d, 8)
        return {"ka_0": a // 2, "ka_1": lax.rem(a, 2)}

    def zz(d):
        return lax.rem(z0 + d + 16, 16)

    def yy(d):
        return lax.rem(y0 + d, 4)

    loads = [
        pltpu.make_async_copy(src, dst, in_sem.at[i])
        for i, (src, dst) in enumerate((
            (orb_hbm.at[:, :, 0:16, :], row),
            (counts_hbm, counts_ref),
            (occ_hbm, occ_ref),
            (cou_hbm, cou),
            (orb_hbm, orb),
            (table_hbm, table_ref),
        ))
    ]
    for load in loads:
        load.start()

    barrier = pltpu.get_barrier_semaphore()
    peers = [zdev(d) for d in (4, -4, 2, -2, 1, -1)] + [ydev(d) for d in (1, 3)] + [adev(d) for d in range(1, 8)]
    for peer in peers:
        pl.semaphore_signal(barrier, inc=1, device_id=peer, device_id_type=MESH)

    lane = lax.broadcasted_iota(jnp.int32, (1, LANES), 1)
    low = lane < HALF
    plus = jnp.where(low, 1.0, -1.0).astype(jnp.float32)
    plus2 = jnp.concatenate([plus, plus], 1)
    low2 = jnp.concatenate([lane, lane], 1) < HALF

    def swap(x):
        return pltpu.roll(x, HALF, 1)

    def swap2(x):
        return jnp.concatenate([swap(x[:, :LANES]), swap(x[:, LANES:])], 1)

    for load in loads[:3]:
        load.wait()
    square = (NKD, NKD)
    on = lax.broadcasted_iota(jnp.int32, square, 0) == lax.broadcasted_iota(jnp.int32, square, 1)
    counts = jnp.sum(jnp.where(on, counts_ref[...].astype(jnp.float32), 0.0), axis=1, keepdims=True)
    band = lax.broadcasted_iota(jnp.int32, (NKD, 3 * LANES), 1).astype(jnp.float32)
    weights = jnp.where(band < counts, occ_ref[...], 0.0)
    for k in range(NKD):
        for c in range(2):
            wide[c * KP + k : c * KP + k + 1, :] = row[k, c, 0:1, :].astype(jnp.float32)
    parts = [wide[c * KP : c * KP + NKD, :] * weights for c in range(2)]
    rest = jnp.where(low, parts[0][:, 256:], swap(parts[1][:, 256:]))
    planes = [parts[0][:, :128], parts[1][:, :128], parts[0][:, 128:256], parts[1][:, 128:256], rest]
    block = jnp.concatenate(planes + [jnp.zeros((RD - PLANES * NKD, LANES), jnp.float32)], 0)
    gath[z0, y0] = block.astype(jnp.bfloat16)

    pl.semaphore_wait(barrier, len(peers))

    def send(src, dst, ssem, rsem, peer):
        return pltpu.make_async_remote_copy(
            src_ref=src, dst_ref=dst, send_sem=ssem, recv_sem=rsem, device_id=peer, device_id_type=MESH
        )

    sent = []

    def go(copy):
        copy.start()
        sent.append(copy)

    def along(o, dz):
        ref, to = gath.at[zz(o), y0], (o - dz) % 16
        return send(ref, ref, sz.at[to], rz.at[to], zdev(dz))

    def chain(o):
        rows, to = (pl.ds(0, CUT), 8) if o > 0 else (pl.ds(CUT, RD - CUT), 16)
        ref = gath.at[zz(o), y0, rows]
        return send(ref, ref, sz.at[to], rz.at[to], zdev(-o))

    def chained(o):
        rows, to = (pl.ds(0, CUT), 8) if o > 0 else (pl.ds(CUT, RD - CUT), 16)
        ref = gath.at[zz(8), y0, rows]
        return send(ref, ref, sz.at[to], rz.at[to], zdev(-o))

    def across(i, o, y):
        ref = gath.at[zz(o), y]
        return send(ref, ref, sy.at[i, o % 16], ry.at[i, o % 16], ydev((1, 3)[i]))

    def onward(o, y):
        ref = gath.at[zz(o), y]
        return send(ref, ref, sf.at[o % 16], rf.at[o % 16], ydev((1, 3)[OFFSETS.index(o) % 2]))

    def near(o):
        for dz in NEAR[o]:
            go(along(o, dz))

    def sides(o):
        for i in range(2):
            go(across(i, o, y0))

    def arrive(o):
        ref = gath.at[zz(o), y0]
        send(ref, ref, sz.at[o % 16], rz.at[o % 16], zdev(1)).wait_recv()
        sides(o)

    def pass_on(o):
        for i in range(2):
            across(i, o, yy((3, 1)[i])).wait_recv()
        go(onward(o, yy((3, 1)[OFFSETS.index(o) % 2])))

    sides(0)
    for dz in (4, -4):
        go(along(0, dz))
    near(0)

    loads[3].wait()
    for k in range(NKD, KP):
        dense[pl.ds(k, 64, stride=KP), :] = jnp.zeros((64, LANES), jnp.float32)

    def lay(k, carry):
        pair = jnp.concatenate([cou[k, 0], cou[k, 1]], axis=1).astype(jnp.float32)
        dense[pl.ds(k, 64, stride=KP), :] = pair
        return carry

    lax.fori_loop(0, NKD, lay, 0)
    vsend[...] = dense[...].astype(jnp.bfloat16).reshape(8, 8, KP, LANES)

    def move(stage, src, dst, d):
        return send(src, dst, sx.at[stage, d - 1], rx.at[stage, d - 1], adev(d))

    def theirs(d):
        return lax.rem(a0 + 8 - d, 8)

    for d in range(1, 8):
        go(move(0, vsend.at[lax.rem(a0 + d, 8)], vrecv.at[:, a0], d))
    vrecv[:, a0] = vsend[a0]

    def turn(k, carry):
        re, im = orb[k, 0], orb[k, 1]
        minus = -im
        rest_re = jnp.where(low, re[:, 256:].astype(jnp.float32), swap(im[:, 256:].astype(jnp.float32)))
        rest_im = jnp.where(low, minus[:, 256:].astype(jnp.float32), swap(re[:, 256:].astype(jnp.float32)))
        right[k, 0:64, :] = jnp.concatenate(
            [re[:, :128], im[:, :128], re[:, 128:256], im[:, 128:256], rest_re.astype(jnp.bfloat16)], 1
        )
        right[k, 64:128, :] = jnp.concatenate(
            [minus[:, :128], re[:, :128], minus[:, 128:256], re[:, 128:256], rest_im.astype(jnp.bfloat16)], 1
        )
        return carry

    def scatter(stage, u, o, y):
        first_group, groups = STAGES[stage]
        base, rows = first_group * 16 * RD, groups * 16
        spread[pl.ds(base + u * 16 + zz(o), RD, stride=rows), :] = gath[zz(o), y].astype(jnp.float32)

    def dens(stage, start, stop):
        first_group, groups = STAGES[stage]
        base, rows = first_group * 16 * RD, groups * 16

        def one(k, carry):
            left = [
                spread[pl.ds(pl.multiple_of(base + (j * NKD + k) * rows, 16), rows), :].astype(jnp.bfloat16)
                for j in range(PLANES)
            ]
            d = lax.dot_general(
                jnp.concatenate(left, 1), right[k], (((1,), (1,)), ((), ())), preferred_element_type=jnp.float32
            )
            dense[pl.ds(first_group * 16 * KP + k, rows, stride=KP), :] = d
            return carry

        lax.fori_loop(start, stop, one, 0, unroll=3)

    def hand_over(stage):
        first_group, groups = STAGES[stage]
        for u in range(first_group, first_group + groups):
            d = dense[u * 16 * KP : (u + 1) * 16 * KP, :].astype(jnp.bfloat16)
            dsend[:, 2 * u : 2 * u + 2] = d.reshape(8, 2, KP, LANES)
        part = pl.ds(2 * first_group, 2 * groups)
        for d in range(1, 8):
            go(move(1 + stage, dsend.at[lax.rem(a0 + d, 8), part], drecv.at[part, a0], d))
        drecv[part, a0] = dsend[a0, part]

    def forward(x):
        y = jnp.dot(table_ref[...], x, preferred_element_type=jnp.float32)
        return y[:PTILE] + (ROOT * plus2) * swap2(y[PTILE:])

    def pair(ref, i, j):
        return jnp.concatenate([ref[i].reshape(PTILE, LANES), ref[j].reshape(PTILE, LANES)], 1)

    def convolve(stage):
        first_group, groups = STAGES[stage]
        part = pl.ds(2 * first_group, 2 * groups)
        for d in range(1, 8):
            move(1 + stage, dsend.at[0, part], drecv.at[part, theirs(d)], d).wait_recv()
        for u in range(first_group, first_group + groups):
            d = forward(pair(drecv, 2 * u, 2 * u + 1))
            y = yy(DELTA_Y[u])
            product = vhat_a[y] * d + vhat_b[y] * swap2(d)
            t = jnp.dot(table_ref[...], product.astype(jnp.bfloat16), preferred_element_type=jnp.float32)
            back = SCALE * t[:PTILE] - (SCALE * ROOT * plus2) * swap2(t[PTILE:])
            back = back.astype(jnp.bfloat16)
            osend[2 * u] = back[:, :LANES].reshape(8, KP, LANES)
            osend[2 * u + 1] = back[:, LANES:].reshape(8, KP, LANES)
        for d in range(1, 8):
            go(move(4 + stage, osend.at[part, lax.rem(a0 + d, 8)], orecv.at[a0, part], d))
        orecv[a0, part] = osend[part, a0]

    def unlay(stage):
        first_group, groups = STAGES[stage]
        part = pl.ds(2 * first_group, 2 * groups)
        for d in range(1, 8):
            move(4 + stage, osend.at[part, 0], orecv.at[theirs(d), part], d).wait_recv()

        def one(a, carry):
            for u in range(first_group, first_group + groups):
                for i in range(2):
                    r = (2 * a + i) * 4 + yy(DELTA_Y[u])
                    spread[pl.ds(r, KP, stride=64), :] = orecv[a, 2 * u + i].astype(jnp.float32)
            return carry

        lax.fori_loop(0, 8, one, 0)

    for o in (-1, 1, -2, 2):
        arrive(o)
    pass_on(0)
    for o in (-4, 4):
        arrive(o)
        go(chain(o))
        near(o)
    loads[4].wait()
    lax.fori_loop(0, 9, turn, 0)
    for o in (-5, 3, -3, 5, -6, 6):
        arrive(o)
    for o in (-1, 1, -2, 2):
        pass_on(o)
    for o in (4, -4):
        chained(o).wait_recv()
    sides(8)
    near(8)
    lax.fori_loop(9, 18, turn, 0)
    for o in (-4, 4):
        pass_on(o)
    for o in (7, -7):
        arrive(o)
    lax.fori_loop(18, NKD, turn, 0)
    for o in OFFSETS[:8]:
        scatter(0, 0, o, y0)
    for o in (-5, 3, -3):
        pass_on(o)
    for o in OFFSETS[8:]:
        scatter(0, 0, o, y0)
    for o in (5, -6, 6):
        pass_on(o)
    for k in range(NKD, KP):
        dense[pl.ds(k, 64, stride=KP), :] = jnp.zeros((64, LANES), jnp.float32)
    dens(0, 0, NKD)
    hand_over(0)
    for o in (8, 7, -7):
        pass_on(o)

    loads[5].wait()
    for d in range(1, 8):
        move(0, vsend.at[0], vrecv.at[:, theirs(d)], d).wait_recv()

    def kern(y):
        v = forward(pair(vrecv, y, y + 4))
        w = swap2(v)
        vhat_a[y] = jnp.where(low2, v, w)
        vhat_b[y] = jnp.where(low2, -w, v)

    for y in range(4):
        kern(y)
    for o in OFFSETS:
        for u in range(2):
            scatter(1, u, o, yy((1, 3)[u]))
    dens(1, 0, NKD)
    hand_over(1)
    convolve(0)
    for o in OFFSETS:
        onward(o, yy(2)).wait_recv()
        scatter(2, 0, o, yy(2))
    dens(2, 0, NKD)
    hand_over(2)
    convolve(1)
    unlay(0)
    convolve(2)
    unlay(1)
    unlay(2)

    def finish(k, carry):
        o = spread[pl.ds(pl.multiple_of(k * 64, 64), 64), :]
        out_ref[k, 0] = o[:, :HALF].astype(jnp.bfloat16)
        out_ref[k, 1] = swap(o)[:, :HALF].astype(jnp.bfloat16)
        return carry

    lax.fori_loop(0, NKD, finish, 0)
    for copy in sent:
        copy.wait_send()


def local(orbitals, counts, occupation, coulomb):
    table = jnp.asarray(transform_table(), jnp.bfloat16)
    bf, f32 = jnp.bfloat16, jnp.float32
    vmem = pltpu.VMEM
    dma = pltpu.SemaphoreType.DMA
    return pl.pallas_call(
        kernel,
        out_shape=jax.ShapeDtypeStruct((NKD, 2, 64, 64), bf),
        in_specs=[pl.BlockSpec(memory_space=pltpu.HBM)] * 5,
        out_specs=pl.BlockSpec(memory_space=vmem),
        scratch_shapes=[
            vmem((NKD, 2, 16, 384), bf),
            vmem((1, NKD), jnp.int32),
            vmem((NKD, 384), f32),
            vmem((NKD, 2, 64, 384), bf),
            vmem((NKD, 2, 64, 64), bf),
            vmem((2 * PTILE, PTILE), bf),
            vmem((NKD, 128, PLANES * LANES), bf),
            vmem((16, 4, RD, LANES), bf),
            vmem((RD * 64, LANES), f32),
            vmem((2 * KP, 384), f32),
            vmem((64 * KP, LANES), f32),
            vmem((8, 8, KP, LANES), bf),
            vmem((8, 8, KP, LANES), bf),
            vmem((4, PTILE, 2 * LANES), f32),
            vmem((4, PTILE, 2 * LANES), f32),
            vmem((8, 8, KP, LANES), bf),
            vmem((8, 8, KP, LANES), bf),
            vmem((8, 8, KP, LANES), bf),
            vmem((8, 8, KP, LANES), bf),
            dma((6,)),
            dma((17,)),
            dma((17,)),
            dma((2, 16)),
            dma((2, 16)),
            dma((16,)),
            dma((16,)),
            dma((7, 7)),
            dma((7, 7)),
        ],
        compiler_params=pltpu.CompilerParams(
            collective_id=0, has_side_effects=True, vmem_limit_bytes=60 * 1024 * 1024
        ),
    )(orbitals, counts.reshape(1, NKD), occupation, coulomb, table)


def solution(mesh):
    finer = Mesh(mesh.devices.reshape(4, 2, 16, 4), ("ka_0", "ka_1", "pts_0", "pts_1"))
    in_specs = (P(KA, None, PTS, None), P(KA), P(KA, None), P(KA, None, None, PTS))
    out_specs = P(KA, None, None, PTS)
    return jax.shard_map(local, mesh=finer, in_specs=in_specs, out_specs=out_specs, check_vma=False)
```

```python
import functools

import jax
import jax.numpy as jnp
import numpy as np
from jax import lax
from jax.experimental import pallas as pl
from jax.experimental.pallas import tpu as pltpu
from jax.sharding import Mesh
from jax.sharding import PartitionSpec as P

KSIDE = 6
PTS = ("pts_0", "pts_1")
KA = ("ka_0", "ka_1")
MESH = pl.DeviceIdType.MESH

NKD = 27
KP = 32
PLANES = 5
RD = 144
LANES = 128
HALF = 64
PTILE = 8 * KP
ROOT = float(np.sqrt(3.0) / 2.0)
SCALE = -1.0 / float(KSIDE**6)

DELTA_Y = (0, 1, 3, 2)
STAGES = ((0, 3), (3, 1))
OFFSETS = (0, -1, 1, -2, 2, -4, 4, -5, 3, -3, 5, -6, 6, 8, 7, -7)
NEAR = {0: (1, -1, 2, -2), -4: (1, -1, 2), 4: (1, -1, -2), 8: (1, -1)}
CUT = 80


def transform_table():
    index = np.arange(KSIDE**3)
    xyz = np.stack([index // 36, index // 6 % 6, index % 6], 1)
    phase = (xyz @ xyz.T) % KSIDE
    cosine = np.array([1.0, 0.5, -0.5, -1.0, -0.5, 0.5])[phase]
    sine = np.array([0.0, 1.0, 1.0, 0.0, -1.0, -1.0])[phase]
    place = index // NKD * KP + index % NKD
    table = np.zeros((2, PTILE, PTILE), np.float32)
    table[0][np.ix_(place, place)] = cosine
    table[1][np.ix_(place, place)] = sine
    return table.reshape(2 * PTILE, PTILE)


def kernel(
    orb_hbm, counts_hbm, occ_hbm, cou_hbm, table_hbm, out_ref,
    row, counts_ref, occ_ref, orb, cou, table_ref,
    right, gath, spread, wide, dense, vsend, vrecv, vhat_a, vhat_b, dsend, drecv, osend, orecv,
    in_sem, sz, rz, sy, ry, sf, rf, sx, rx,
):
    z0, y0 = lax.axis_index("pts_0"), lax.axis_index("pts_1")
    a0 = lax.axis_index("ka_0") * 2 + lax.axis_index("ka_1")

    def zdev(d):
        return {"pts_0": lax.rem(z0 + d + 16, 16)}

    def ydev(d):
        return {"pts_1": lax.rem(y0 + d, 4)}

    def adev(d):
        a = lax.rem(a0 + d, 8)
        return {"ka_0": a // 2, "ka_1": lax.rem(a, 2)}

    def zz(d):
        return lax.rem(z0 + d + 16, 16)

    def yy(d):
        return lax.rem(y0 + d, 4)

    loads = [
        pltpu.make_async_copy(src, dst, in_sem.at[i])
        for i, (src, dst) in enumerate((
            (orb_hbm.at[:, :, 0:16, :], row),
            (counts_hbm, counts_ref),
            (occ_hbm, occ_ref),
            (cou_hbm, cou),
            (orb_hbm, orb),
            (table_hbm, table_ref),
        ))
    ]
    for load in loads:
        load.start()

    barrier = pltpu.get_barrier_semaphore()
    peers = [zdev(d) for d in (4, -4, 2, -2, 1, -1)] + [ydev(d) for d in (1, 3)] + [adev(d) for d in range(1, 8)]
    for peer in peers:
        pl.semaphore_signal(barrier, inc=1, device_id=peer, device_id_type=MESH)

    lane = lax.broadcasted_iota(jnp.int32, (1, LANES), 1)
    low = lane < HALF
    plus = jnp.where(low, 1.0, -1.0).astype(jnp.float32)
    plus2 = jnp.concatenate([plus, plus], 1)
    low2 = jnp.concatenate([lane, lane], 1) < HALF

    def swap(x):
        return pltpu.roll(x, HALF, 1)

    def swap2(x):
        return jnp.concatenate([swap(x[:, :LANES]), swap(x[:, LANES:])], 1)

    for load in loads[:3]:
        load.wait()
    square = (NKD, NKD)
    on = lax.broadcasted_iota(jnp.int32, square, 0) == lax.broadcasted_iota(jnp.int32, square, 1)
    counts = jnp.sum(jnp.where(on, counts_ref[...].astype(jnp.float32), 0.0), axis=1, keepdims=True)
    band = lax.broadcasted_iota(jnp.int32, (NKD, 3 * LANES), 1).astype(jnp.float32)
    weights = jnp.where(band < counts, occ_ref[...], 0.0)
    for k in range(NKD):
        for c in range(2):
            wide[c * KP + k : c * KP + k + 1, :] = row[k, c, 0:1, :].astype(jnp.float32)
    parts = [wide[c * KP : c * KP + NKD, :] * weights for c in range(2)]
    rest = jnp.where(low, parts[0][:, 256:], swap(parts[1][:, 256:]))
    planes = [parts[0][:, :128], parts[1][:, :128], parts[0][:, 128:256], parts[1][:, 128:256], rest]
    block = jnp.concatenate(planes + [jnp.zeros((RD - PLANES * NKD, LANES), jnp.float32)], 0)
    gath[z0, y0] = block.astype(jnp.bfloat16)

    pl.semaphore_wait(barrier, len(peers))

    def send(src, dst, ssem, rsem, peer):
        return pltpu.make_async_remote_copy(
            src_ref=src, dst_ref=dst, send_sem=ssem, recv_sem=rsem, device_id=peer, device_id_type=MESH
        )

    sent = []

    def go(copy):
        copy.start()
        sent.append(copy)

    def along(o, dz):
        ref, to = gath.at[zz(o), y0], (o - dz) % 16
        return send(ref, ref, sz.at[to], rz.at[to], zdev(dz))

    def chain(o):
        rows, to = (pl.ds(0, CUT), 8) if o > 0 else (pl.ds(CUT, RD - CUT), 16)
        ref = gath.at[zz(o), y0, rows]
        return send(ref, ref, sz.at[to], rz.at[to], zdev(-o))

    def chained(o):
        rows, to = (pl.ds(0, CUT), 8) if o > 0 else (pl.ds(CUT, RD - CUT), 16)
        ref = gath.at[zz(8), y0, rows]
        return send(ref, ref, sz.at[to], rz.at[to], zdev(-o))

    def across(i, o, y):
        ref = gath.at[zz(o), y]
        return send(ref, ref, sy.at[i, o % 16], ry.at[i, o % 16], ydev((1, 3)[i]))

    def onward(o, y):
        ref = gath.at[zz(o), y]
        return send(ref, ref, sf.at[o % 16], rf.at[o % 16], ydev((1, 3)[OFFSETS.index(o) % 2]))

    def near(o):
        for dz in NEAR[o]:
            go(along(o, dz))

    def sides(o):
        for i in range(2):
            go(across(i, o, y0))

    def arrive(o):
        ref = gath.at[zz(o), y0]
        send(ref, ref, sz.at[o % 16], rz.at[o % 16], zdev(1)).wait_recv()
        sides(o)

    def pass_on(o):
        for i in range(2):
            across(i, o, yy((3, 1)[i])).wait_recv()
        go(onward(o, yy((3, 1)[OFFSETS.index(o) % 2])))

    sides(0)
    for dz in (4, -4):
        go(along(0, dz))
    near(0)

    loads[3].wait()
    for k in range(NKD, KP):
        dense[pl.ds(k, 64, stride=KP), :] = jnp.zeros((64, LANES), jnp.float32)

    def lay(k, carry):
        pair = jnp.concatenate([cou[k, 0], cou[k, 1]], axis=1).astype(jnp.float32)
        dense[pl.ds(k, 64, stride=KP), :] = pair
        return carry

    lax.fori_loop(0, NKD, lay, 0)
    vsend[...] = dense[...].astype(jnp.bfloat16).reshape(8, 8, KP, LANES)

    def move(stage, src, dst, d):
        return send(src, dst, sx.at[stage, d - 1], rx.at[stage, d - 1], adev(d))

    def theirs(d):
        return lax.rem(a0 + 8 - d, 8)

    for d in range(1, 8):
        go(move(0, vsend.at[lax.rem(a0 + d, 8)], vrecv.at[:, a0], d))
    vrecv[:, a0] = vsend[a0]

    def turn(k, carry):
        re, im = orb[k, 0], orb[k, 1]
        minus = -im
        rest_re = jnp.where(low, re[:, 256:].astype(jnp.float32), swap(im[:, 256:].astype(jnp.float32)))
        rest_im = jnp.where(low, minus[:, 256:].astype(jnp.float32), swap(re[:, 256:].astype(jnp.float32)))
        right[k, 0:64, :] = jnp.concatenate(
            [re[:, :128], im[:, :128], re[:, 128:256], im[:, 128:256], rest_re.astype(jnp.bfloat16)], 1
        )
        right[k, 64:128, :] = jnp.concatenate(
            [minus[:, :128], re[:, :128], minus[:, 128:256], re[:, 128:256], rest_im.astype(jnp.bfloat16)], 1
        )
        return carry

    def scatter(stage, start, count, us):
        first_group, groups = STAGES[stage]
        base, rows = first_group * 16 * RD, groups * 16

        def one(i, carry):
            z = lax.rem(z0 + start + i, 16)
            for u in us:
                y = yy(DELTA_Y[first_group + u])
                spread[pl.ds(base + u * 16 + z, RD, stride=rows), :] = gath[z, y].astype(jnp.float32)
            return carry

        lax.fori_loop(0, count, one, 0)

    def dens(stage, start, stop):
        first_group, groups = STAGES[stage]
        base, rows = first_group * 16 * RD, groups * 16

        def one(k, carry):
            left = [
                spread[pl.ds(pl.multiple_of(base + (j * NKD + k) * rows, 16), rows), :].astype(jnp.bfloat16)
                for j in range(PLANES)
            ]
            d = lax.dot_general(
                jnp.concatenate(left, 1), right[k], (((1,), (1,)), ((), ())), preferred_element_type=jnp.float32
            )
            dense[pl.ds(first_group * 16 * KP + k, rows, stride=KP), :] = d
            return carry

        lax.fori_loop(start, stop, one, 0, unroll=3)

    def hand_over(stage):
        first_group, groups = STAGES[stage]
        for u in range(first_group, first_group + groups):
            d = dense[u * 16 * KP : (u + 1) * 16 * KP, :].astype(jnp.bfloat16)
            dsend[:, 2 * u : 2 * u + 2] = d.reshape(8, 2, KP, LANES)
        part = pl.ds(2 * first_group, 2 * groups)
        for d in range(1, 8):
            go(move(1 + stage, dsend.at[lax.rem(a0 + d, 8), part], drecv.at[part, a0], d))
        drecv[part, a0] = dsend[a0, part]

    def forward(x):
        y = jnp.dot(table_ref[...], x, preferred_element_type=jnp.float32)
        return y[:PTILE] + (ROOT * plus2) * swap2(y[PTILE:])

    def pair(ref, i, j):
        return jnp.concatenate([ref[i].reshape(PTILE, LANES), ref[j].reshape(PTILE, LANES)], 1)

    def convolve(stage):
        first_group, groups = STAGES[stage]
        part = pl.ds(2 * first_group, 2 * groups)
        for d in range(1, 8):
            move(1 + stage, dsend.at[0, part], drecv.at[part, theirs(d)], d).wait_recv()
        for u in range(first_group, first_group + groups):
            d = forward(pair(drecv, 2 * u, 2 * u + 1))
            y = yy(DELTA_Y[u])
            product = vhat_a[y] * d + vhat_b[y] * swap2(d)
            t = jnp.dot(table_ref[...], product.astype(jnp.bfloat16), preferred_element_type=jnp.float32)
            back = SCALE * t[:PTILE] - (SCALE * ROOT * plus2) * swap2(t[PTILE:])
            back = back.astype(jnp.bfloat16)
            osend[2 * u] = back[:, :LANES].reshape(8, KP, LANES)
            osend[2 * u + 1] = back[:, LANES:].reshape(8, KP, LANES)
        for d in range(1, 8):
            go(move(4 + stage, osend.at[part, lax.rem(a0 + d, 8)], orecv.at[a0, part], d))
        orecv[a0, part] = osend[part, a0]

    def unlay(stage):
        first_group, groups = STAGES[stage]
        part = pl.ds(2 * first_group, 2 * groups)
        for d in range(1, 8):
            move(4 + stage, osend.at[part, 0], orecv.at[theirs(d), part], d).wait_recv()

        def one(a, carry):
            for u in range(first_group, first_group + groups):
                for i in range(2):
                    r = (2 * a + i) * 4 + yy(DELTA_Y[u])
                    spread[pl.ds(r, KP, stride=64), :] = orecv[a, 2 * u + i].astype(jnp.float32)
            return carry

        lax.fori_loop(0, 8, one, 0)

    for o in (-1, 1, -2, 2):
        arrive(o)
    pass_on(0)
    for o in (-4, 4):
        arrive(o)
        go(chain(o))
        near(o)
    loads[4].wait()
    lax.fori_loop(0, 9, turn, 0)
    for o in (-5, 3, -3, 5, -6, 6):
        arrive(o)
    for o in (-1, 1, -2, 2):
        pass_on(o)
    for o in (4, -4):
        chained(o).wait_recv()
    sides(8)
    near(8)
    lax.fori_loop(9, 18, turn, 0)
    for o in (-4, 4):
        pass_on(o)
    for o in (7, -7):
        arrive(o)
    lax.fori_loop(18, NKD, turn, 0)
    scatter(0, 10, 7, (0,))
    for o in (-5, 3, -3):
        pass_on(o)
    scatter(0, 1, 9, (0,))
    for o in (5, -6, 6):
        pass_on(o)
    for k in range(NKD, KP):
        dense[pl.ds(k, 64, stride=KP), :] = jnp.zeros((64, LANES), jnp.float32)
    for o in (8, 7, -7):
        pass_on(o)

    loads[5].wait()
    for d in range(1, 8):
        move(0, vsend.at[0], vrecv.at[:, theirs(d)], d).wait_recv()

    def kern(y):
        v = forward(pair(vrecv, y, y + 4))
        w = swap2(v)
        vhat_a[y] = jnp.where(low2, v, w)
        vhat_b[y] = jnp.where(low2, -w, v)

    for y in range(4):
        kern(y)
    scatter(0, 0, 16, (1, 2))
    dens(0, 0, NKD)
    hand_over(0)
    for o in OFFSETS[:13]:
        onward(o, yy(2)).wait_recv()
    scatter(1, 10, 13, (0,))
    for o in OFFSETS[13:]:
        onward(o, yy(2)).wait_recv()
    scatter(1, 7, 3, (0,))
    dens(1, 0, NKD)
    hand_over(1)
    convolve(0)
    convolve(1)
    unlay(0)
    unlay(1)

    def finish(k, carry):
        o = spread[pl.ds(pl.multiple_of(k * 64, 64), 64), :]
        out_ref[k, 0] = o[:, :HALF].astype(jnp.bfloat16)
        out_ref[k, 1] = swap(o)[:, :HALF].astype(jnp.bfloat16)
        return carry

    lax.fori_loop(0, NKD, finish, 0)
    for copy in sent:
        copy.wait_send()


def local(orbitals, counts, occupation, coulomb):
    table = jnp.asarray(transform_table(), jnp.bfloat16)
    bf, f32 = jnp.bfloat16, jnp.float32
    vmem = pltpu.VMEM
    dma = pltpu.SemaphoreType.DMA
    return pl.pallas_call(
        kernel,
        out_shape=jax.ShapeDtypeStruct((NKD, 2, 64, 64), bf),
        in_specs=[pl.BlockSpec(memory_space=pltpu.HBM)] * 5,
        out_specs=pl.BlockSpec(memory_space=vmem),
        scratch_shapes=[
            vmem((NKD, 2, 16, 384), bf),
            vmem((1, NKD), jnp.int32),
            vmem((NKD, 384), f32),
            vmem((NKD, 2, 64, 384), bf),
            vmem((NKD, 2, 64, 64), bf),
            vmem((2 * PTILE, PTILE), bf),
            vmem((NKD, 128, PLANES * LANES), bf),
            vmem((16, 4, RD, LANES), bf),
            vmem((RD * 64, LANES), f32),
            vmem((2 * KP, 384), f32),
            vmem((64 * KP, LANES), f32),
            vmem((8, 8, KP, LANES), bf),
            vmem((8, 8, KP, LANES), bf),
            vmem((4, PTILE, 2 * LANES), f32),
            vmem((4, PTILE, 2 * LANES), f32),
            vmem((8, 8, KP, LANES), bf),
            vmem((8, 8, KP, LANES), bf),
            vmem((8, 8, KP, LANES), bf),
            vmem((8, 8, KP, LANES), bf),
            dma((6,)),
            dma((17,)),
            dma((17,)),
            dma((2, 16)),
            dma((2, 16)),
            dma((16,)),
            dma((16,)),
            dma((7, 7)),
            dma((7, 7)),
        ],
        compiler_params=pltpu.CompilerParams(
            collective_id=0, has_side_effects=True, vmem_limit_bytes=60 * 1024 * 1024
        ),
    )(orbitals, counts.reshape(1, NKD), occupation, coulomb, table)


def solution(mesh):
    finer = Mesh(mesh.devices.reshape(4, 2, 16, 4), ("ka_0", "ka_1", "pts_0", "pts_1"))
    in_specs = (P(KA, None, PTS, None), P(KA), P(KA, None), P(KA, None, None, PTS))
    out_specs = P(KA, None, None, PTS)
    return jax.shard_map(local, mesh=finer, in_specs=in_specs, out_specs=out_specs, check_vma=False)
```

```python
import functools

import jax
import jax.numpy as jnp
import numpy as np
from jax import lax
from jax.experimental import pallas as pl
from jax.experimental.pallas import tpu as pltpu
from jax.sharding import Mesh
from jax.sharding import PartitionSpec as P

KSIDE = 6
PTS = ("pts_0", "pts_1")
KA = ("ka_0", "ka_1")
MESH = pl.DeviceIdType.MESH

NKD = 27
KP = 32
PLANES = 5
RD = 144
LANES = 128
HALF = 64
PTILE = 8 * KP
ROOT = float(np.sqrt(3.0) / 2.0)
SCALE = -1.0 / float(KSIDE**6)

DELTA_Y = (0, 1, 3, 2)
STAGES = ((0, 1), (1, 2), (3, 1))
OFFSETS = (0, -1, 1, -2, 2, -4, 4, -5, 3, -3, 5, -6, 6, 8, 7, -7)
NEAR = {0: (1, -1, 2, -2), -4: (1, -1, 2), 4: (1, -1, -2), 8: (1, -1)}
CUT = 80


def transform_table():
    index = np.arange(KSIDE**3)
    xyz = np.stack([index // 36, index // 6 % 6, index % 6], 1)
    phase = (xyz @ xyz.T) % KSIDE
    cosine = np.array([1.0, 0.5, -0.5, -1.0, -0.5, 0.5])[phase]
    sine = np.array([0.0, 1.0, 1.0, 0.0, -1.0, -1.0])[phase]
    place = index // NKD * KP + index % NKD
    table = np.zeros((2, PTILE, PTILE), np.float32)
    table[0][np.ix_(place, place)] = cosine
    table[1][np.ix_(place, place)] = sine
    return table.reshape(2 * PTILE, PTILE)


def kernel(
    orb_hbm, counts_hbm, occ_hbm, cou_hbm, table_hbm, out_ref,
    row, counts_ref, occ_ref, orb, cou, table_ref,
    right, gath, spread, wide, dense, vsend, vrecv, vhat_a, vhat_b, dsend, drecv, osend, orecv,
    in_sem, sz, rz, sy, ry, sf, rf, sx, rx,
):
    z0, y0 = lax.axis_index("pts_0"), lax.axis_index("pts_1")
    a0 = lax.axis_index("ka_0") * 2 + lax.axis_index("ka_1")

    def zdev(d):
        return {"pts_0": lax.rem(z0 + d + 16, 16)}

    def ydev(d):
        return {"pts_1": lax.rem(y0 + d, 4)}

    def adev(d):
        a = lax.rem(a0 + d, 8)
        return {"ka_0": a // 2, "ka_1": lax.rem(a, 2)}

    def zz(d):
        return lax.rem(z0 + d + 16, 16)

    def yy(d):
        return lax.rem(y0 + d, 4)

    loads = [
        pltpu.make_async_copy(src, dst, in_sem.at[i])
        for i, (src, dst) in enumerate((
            (orb_hbm.at[:, :, 0:16, :], row),
            (counts_hbm, counts_ref),
            (occ_hbm, occ_ref),
            (cou_hbm, cou),
            (orb_hbm, orb),
            (table_hbm, table_ref),
        ))
    ]
    for load in loads:
        load.start()

    barrier = pltpu.get_barrier_semaphore()
    peers = [zdev(d) for d in (4, -4, 2, -2, 1, -1)] + [ydev(d) for d in (1, 3)] + [adev(d) for d in range(1, 8)]
    for peer in peers:
        pl.semaphore_signal(barrier, inc=1, device_id=peer, device_id_type=MESH)

    lane = lax.broadcasted_iota(jnp.int32, (1, LANES), 1)
    low = lane < HALF
    plus = jnp.where(low, 1.0, -1.0).astype(jnp.float32)
    plus2 = jnp.concatenate([plus, plus], 1)
    low2 = jnp.concatenate([lane, lane], 1) < HALF

    def swap(x):
        return pltpu.roll(x, HALF, 1)

    def swap2(x):
        return jnp.concatenate([swap(x[:, :LANES]), swap(x[:, LANES:])], 1)

    for load in loads[:3]:
        load.wait()
    square = (NKD, NKD)
    on = lax.broadcasted_iota(jnp.int32, square, 0) == lax.broadcasted_iota(jnp.int32, square, 1)
    counts = jnp.sum(jnp.where(on, counts_ref[...].astype(jnp.float32), 0.0), axis=1, keepdims=True)
    band = lax.broadcasted_iota(jnp.int32, (NKD, 3 * LANES), 1).astype(jnp.float32)
    weights = jnp.where(band < counts, occ_ref[...], 0.0)
    for k in range(NKD):
        for c in range(2):
            wide[c * KP + k : c * KP + k + 1, :] = row[k, c, 0:1, :].astype(jnp.float32)
    parts = [wide[c * KP : c * KP + NKD, :] * weights for c in range(2)]
    rest = jnp.where(low, parts[0][:, 256:], swap(parts[1][:, 256:]))
    planes = [parts[0][:, :128], parts[1][:, :128], parts[0][:, 128:256], parts[1][:, 128:256], rest]
    block = jnp.concatenate(planes + [jnp.zeros((RD - PLANES * NKD, LANES), jnp.float32)], 0)
    gath[z0, y0] = block.astype(jnp.bfloat16)

    pl.semaphore_wait(barrier, len(peers))

    def send(src, dst, ssem, rsem, peer):
        return pltpu.make_async_remote_copy(
            src_ref=src, dst_ref=dst, send_sem=ssem, recv_sem=rsem, device_id=peer, device_id_type=MESH
        )

    sent = []

    def go(copy):
        copy.start()
        sent.append(copy)

    def along(o, dz):
        ref, to = gath.at[zz(o), y0], (o - dz) % 16
        return send(ref, ref, sz.at[to], rz.at[to], zdev(dz))

    def chain(o):
        rows, to = (pl.ds(0, CUT), 8) if o > 0 else (pl.ds(CUT, RD - CUT), 16)
        ref = gath.at[zz(o), y0, rows]
        return send(ref, ref, sz.at[to], rz.at[to], zdev(-o))

    def chained(o):
        rows, to = (pl.ds(0, CUT), 8) if o > 0 else (pl.ds(CUT, RD - CUT), 16)
        ref = gath.at[zz(8), y0, rows]
        return send(ref, ref, sz.at[to], rz.at[to], zdev(-o))

    def across(i, o, y):
        ref = gath.at[zz(o), y]
        return send(ref, ref, sy.at[i, o % 16], ry.at[i, o % 16], ydev((1, 3)[i]))

    def onward(o, y):
        ref = gath.at[zz(o), y]
        return send(ref, ref, sf.at[o % 16], rf.at[o % 16], ydev((1, 3)[OFFSETS.index(o) % 2]))

    def near(o):
        for dz in NEAR[o]:
            go(along(o, dz))

    def sides(o):
        for i in range(2):
            go(across(i, o, y0))

    def arrive(o):
        ref = gath.at[zz(o), y0]
        send(ref, ref, sz.at[o % 16], rz.at[o % 16], zdev(1)).wait_recv()
        sides(o)

    def pass_on(o):
        for i in range(2):
            across(i, o, yy((3, 1)[i])).wait_recv()
        go(onward(o, yy((3, 1)[OFFSETS.index(o) % 2])))

    sides(0)
    for dz in (4, -4):
        go(along(0, dz))
    near(0)

    loads[3].wait()
    for k in range(NKD, KP):
        dense[pl.ds(k, 64, stride=KP), :] = jnp.zeros((64, LANES), jnp.float32)

    def lay(k, carry):
        pair = jnp.concatenate([cou[k, 0], cou[k, 1]], axis=1).astype(jnp.float32)
        dense[pl.ds(k, 64, stride=KP), :] = pair
        return carry

    lax.fori_loop(0, NKD, lay, 0, unroll=9)
    vsend[...] = dense[...].astype(jnp.bfloat16).reshape(8, 8, KP, LANES)

    def move(stage, src, dst, d):
        return send(src, dst, sx.at[stage, d - 1], rx.at[stage, d - 1], adev(d))

    def theirs(d):
        return lax.rem(a0 + 8 - d, 8)

    for d in range(1, 8):
        go(move(0, vsend.at[lax.rem(a0 + d, 8)], vrecv.at[:, a0], d))
    vrecv[:, a0] = vsend[a0]

    def turn(k, carry):
        re, im = orb[k, 0], orb[k, 1]
        minus = -im
        rest_re = jnp.where(low, re[:, 256:].astype(jnp.float32), swap(im[:, 256:].astype(jnp.float32)))
        rest_im = jnp.where(low, minus[:, 256:].astype(jnp.float32), swap(re[:, 256:].astype(jnp.float32)))
        right[k, 0:64, :] = jnp.concatenate(
            [re[:, :128], im[:, :128], re[:, 128:256], im[:, 128:256], rest_re.astype(jnp.bfloat16)], 1
        )
        right[k, 64:128, :] = jnp.concatenate(
            [minus[:, :128], re[:, :128], minus[:, 128:256], re[:, 128:256], rest_im.astype(jnp.bfloat16)], 1
        )
        return carry

    def scatter(stage, start, count):
        first_group, groups = STAGES[stage]
        base, rows = first_group * 16 * RD, groups * 16

        def one(i, carry):
            z = lax.rem(z0 + start + i, 16)
            for u in range(groups):
                y = yy(DELTA_Y[first_group + u])
                spread[pl.ds(base + u * 16 + z, RD, stride=rows), :] = gath[z, y].astype(jnp.float32)
            return carry

        lax.fori_loop(0, count, one, 0)

    def dens(stage, start, stop):
        first_group, groups = STAGES[stage]
        base, rows = first_group * 16 * RD, groups * 16

        def one(k, carry):
            left = [
                spread[pl.ds(pl.multiple_of(base + (j * NKD + k) * rows, 16), rows), :].astype(jnp.bfloat16)
                for j in range(PLANES)
            ]
            d = lax.dot_general(
                jnp.concatenate(left, 1), right[k], (((1,), (1,)), ((), ())), preferred_element_type=jnp.float32
            )
            dense[pl.ds(first_group * 16 * KP + k, rows, stride=KP), :] = d
            return carry

        lax.fori_loop(start, stop, one, 0, unroll=9)

    def hand_over(stage):
        first_group, groups = STAGES[stage]
        for u in range(first_group, first_group + groups):
            d = dense[u * 16 * KP : (u + 1) * 16 * KP, :].astype(jnp.bfloat16)
            dsend[:, 2 * u : 2 * u + 2] = d.reshape(8, 2, KP, LANES)
        part = pl.ds(2 * first_group, 2 * groups)
        for d in range(1, 8):
            go(move(1 + stage, dsend.at[lax.rem(a0 + d, 8), part], drecv.at[part, a0], d))
        drecv[part, a0] = dsend[a0, part]

    def forward(x):
        y = jnp.dot(table_ref[...], x, preferred_element_type=jnp.float32)
        return y[:PTILE] + (ROOT * plus2) * swap2(y[PTILE:])

    def pair(ref, i, j):
        return jnp.concatenate([ref[i].reshape(PTILE, LANES), ref[j].reshape(PTILE, LANES)], 1)

    def convolve(stage):
        first_group, groups = STAGES[stage]
        part = pl.ds(2 * first_group, 2 * groups)
        for d in range(1, 8):
            move(1 + stage, dsend.at[0, part], drecv.at[part, theirs(d)], d).wait_recv()
        for u in range(first_group, first_group + groups):
            d = forward(pair(drecv, 2 * u, 2 * u + 1))
            y = yy(DELTA_Y[u])
            product = vhat_a[y] * d + vhat_b[y] * swap2(d)
            t = jnp.dot(table_ref[...], product.astype(jnp.bfloat16), preferred_element_type=jnp.float32)
            back = SCALE * t[:PTILE] - (SCALE * ROOT * plus2) * swap2(t[PTILE:])
            back = back.astype(jnp.bfloat16)
            osend[2 * u] = back[:, :LANES].reshape(8, KP, LANES)
            osend[2 * u + 1] = back[:, LANES:].reshape(8, KP, LANES)
        for d in range(1, 8):
            go(move(4 + stage, osend.at[part, lax.rem(a0 + d, 8)], orecv.at[a0, part], d))
        orecv[a0, part] = osend[part, a0]

    def unlay(stage):
        first_group, groups = STAGES[stage]
        part = pl.ds(2 * first_group, 2 * groups)
        for d in range(1, 8):
            move(4 + stage, osend.at[part, 0], orecv.at[theirs(d), part], d).wait_recv()

        def one(a, carry):
            for u in range(first_group, first_group + groups):
                for i in range(2):
                    r = (2 * a + i) * 4 + yy(DELTA_Y[u])
                    spread[pl.ds(r, KP, stride=64), :] = orecv[a, 2 * u + i].astype(jnp.float32)
            return carry

        lax.fori_loop(0, 8, one, 0, unroll=2)

    for o in (-1, 1, -2, 2):
        arrive(o)
    pass_on(0)
    for o in (-4, 4):
        arrive(o)
        go(chain(o))
        near(o)
    loads[4].wait()
    lax.fori_loop(0, 9, turn, 0, unroll=3)
    for o in (-5, 3, -3, 5, -6, 6):
        arrive(o)
    for o in (-1, 1, -2, 2):
        pass_on(o)
    for o in (4, -4):
        chained(o).wait_recv()
    sides(8)
    near(8)
    lax.fori_loop(9, 18, turn, 0, unroll=3)
    for o in (-4, 4):
        pass_on(o)
    for o in (7, -7):
        arrive(o)
    lax.fori_loop(18, NKD, turn, 0, unroll=3)
    scatter(0, 10, 7)
    for o in (-5, 3, -3):
        pass_on(o)
    scatter(0, 1, 9)
    for o in (5, -6, 6):
        pass_on(o)
    for k in range(NKD, KP):
        dense[pl.ds(k, 64, stride=KP), :] = jnp.zeros((64, LANES), jnp.float32)
    dens(0, 0, NKD)
    hand_over(0)
    for o in (8, 7, -7):
        pass_on(o)

    loads[5].wait()
    for d in range(1, 8):
        move(0, vsend.at[0], vrecv.at[:, theirs(d)], d).wait_recv()

    def kern(y):
        v = forward(pair(vrecv, y, y + 4))
        w = swap2(v)
        vhat_a[y] = jnp.where(low2, v, w)
        vhat_b[y] = jnp.where(low2, -w, v)

    for y in range(4):
        kern(y)
    scatter(1, 0, 16)
    dens(1, 0, NKD)
    hand_over(1)
    convolve(0)
    for o in OFFSETS[:13]:
        onward(o, yy(2)).wait_recv()
    scatter(2, 10, 13)
    for o in OFFSETS[13:]:
        onward(o, yy(2)).wait_recv()
    scatter(2, 7, 3)
    dens(2, 0, NKD)
    hand_over(2)
    convolve(1)
    unlay(0)
    convolve(2)
    unlay(1)
    unlay(2)

    def finish(k, carry):
        o = spread[pl.ds(pl.multiple_of(k * 64, 64), 64), :]
        out_ref[k, 0] = o[:, :HALF].astype(jnp.bfloat16)
        out_ref[k, 1] = swap(o)[:, :HALF].astype(jnp.bfloat16)
        return carry

    lax.fori_loop(0, NKD, finish, 0, unroll=9)
    for copy in sent:
        copy.wait_send()


def local(orbitals, counts, occupation, coulomb):
    table = jnp.asarray(transform_table(), jnp.bfloat16)
    bf, f32 = jnp.bfloat16, jnp.float32
    vmem = pltpu.VMEM
    dma = pltpu.SemaphoreType.DMA
    return pl.pallas_call(
        kernel,
        out_shape=jax.ShapeDtypeStruct((NKD, 2, 64, 64), bf),
        in_specs=[pl.BlockSpec(memory_space=pltpu.HBM)] * 5,
        out_specs=pl.BlockSpec(memory_space=vmem),
        scratch_shapes=[
            vmem((NKD, 2, 16, 384), bf),
            vmem((1, NKD), jnp.int32),
            vmem((NKD, 384), f32),
            vmem((NKD, 2, 64, 384), bf),
            vmem((NKD, 2, 64, 64), bf),
            vmem((2 * PTILE, PTILE), bf),
            vmem((NKD, 128, PLANES * LANES), bf),
            vmem((16, 4, RD, LANES), bf),
            vmem((RD * 64, LANES), f32),
            vmem((2 * KP, 384), f32),
            vmem((64 * KP, LANES), f32),
            vmem((8, 8, KP, LANES), bf),
            vmem((8, 8, KP, LANES), bf),
            vmem((4, PTILE, 2 * LANES), f32),
            vmem((4, PTILE, 2 * LANES), f32),
            vmem((8, 8, KP, LANES), bf),
            vmem((8, 8, KP, LANES), bf),
            vmem((8, 8, KP, LANES), bf),
            vmem((8, 8, KP, LANES), bf),
            dma((6,)),
            dma((17,)),
            dma((17,)),
            dma((2, 16)),
            dma((2, 16)),
            dma((16,)),
            dma((16,)),
            dma((7, 7)),
            dma((7, 7)),
        ],
        compiler_params=pltpu.CompilerParams(
            collective_id=0, has_side_effects=True, vmem_limit_bytes=60 * 1024 * 1024
        ),
    )(orbitals, counts.reshape(1, NKD), occupation, coulomb, table)


def solution(mesh):
    finer = Mesh(mesh.devices.reshape(4, 2, 16, 4), ("ka_0", "ka_1", "pts_0", "pts_1"))
    in_specs = (P(KA, None, PTS, None), P(KA), P(KA, None), P(KA, None, None, PTS))
    out_specs = P(KA, None, None, PTS)
    return jax.shard_map(local, mesh=finer, in_specs=in_specs, out_specs=out_specs, check_vma=False)
```

```python
import functools

import jax
import jax.numpy as jnp
import numpy as np
from jax import lax
from jax.experimental import pallas as pl
from jax.experimental.pallas import tpu as pltpu
from jax.sharding import Mesh
from jax.sharding import PartitionSpec as P

KSIDE = 6
PTS = ("pts_0", "pts_1")
KA = ("ka_0", "ka_1")
MESH = pl.DeviceIdType.MESH

NKD = 27
KP = 32
PLANES = 5
RD = 144
LANES = 128
HALF = 64
PTILE = 8 * KP
ROOT = float(np.sqrt(3.0) / 2.0)
SCALE = -1.0 / float(KSIDE**6)

DELTA_Y = (0, 1, 3, 2)
STAGES = ((0, 1), (1, 2), (3, 1))
OFFSETS = (0, -1, 1, -2, 2, -4, 4, -5, 3, -3, 5, -6, 6, 8, 7, -7)
NEAR = {0: (1, -1, 2, -2), -4: (1, -1, 2), 4: (1, -1, -2), 8: (1, -1)}
CUT = 80


def transform_table():
    index = np.arange(KSIDE**3)
    xyz = np.stack([index // 36, index // 6 % 6, index % 6], 1)
    phase = (xyz @ xyz.T) % KSIDE
    cosine = np.array([1.0, 0.5, -0.5, -1.0, -0.5, 0.5])[phase]
    sine = np.array([0.0, 1.0, 1.0, 0.0, -1.0, -1.0])[phase]
    place = index // NKD * KP + index % NKD
    table = np.zeros((2, PTILE, PTILE), np.float32)
    table[0][np.ix_(place, place)] = cosine
    table[1][np.ix_(place, place)] = sine
    return table.reshape(2 * PTILE, PTILE)


def kernel(
    orb_hbm, counts_hbm, occ_hbm, cou_hbm, table_hbm, out_ref,
    row, counts_ref, occ_ref, orb, cou, table_ref,
    right, gath, spread, wide, dense, vsend, vrecv, vhat_a, vhat_b, dsend, drecv, osend, orecv,
    in_sem, sz, rz, sy, ry, sf, rf, sx, rx,
):
    z0, y0 = lax.axis_index("pts_0"), lax.axis_index("pts_1")
    a0 = lax.axis_index("ka_0") * 2 + lax.axis_index("ka_1")

    def zdev(d):
        return {"pts_0": lax.rem(z0 + d + 16, 16)}

    def ydev(d):
        return {"pts_1": lax.rem(y0 + d, 4)}

    def adev(d):
        a = lax.rem(a0 + d, 8)
        return {"ka_0": a // 2, "ka_1": lax.rem(a, 2)}

    def zz(d):
        return lax.rem(z0 + d + 16, 16)

    def yy(d):
        return lax.rem(y0 + d, 4)

    loads = [
        pltpu.make_async_copy(src, dst, in_sem.at[i])
        for i, (src, dst) in enumerate((
            (orb_hbm.at[:, :, 0:16, :], row),
            (counts_hbm, counts_ref),
            (occ_hbm, occ_ref),
            (cou_hbm, cou),
            (orb_hbm, orb),
            (table_hbm, table_ref),
        ))
    ]
    for load in loads:
        load.start()

    barrier = pltpu.get_barrier_semaphore()
    peers = [zdev(d) for d in (4, -4, 2, -2, 1, -1)] + [ydev(d) for d in (1, 3)] + [adev(d) for d in range(1, 8)]
    for peer in peers:
        pl.semaphore_signal(barrier, inc=1, device_id=peer, device_id_type=MESH)

    lane = lax.broadcasted_iota(jnp.int32, (1, LANES), 1)
    low = lane < HALF
    plus = jnp.where(low, 1.0, -1.0).astype(jnp.float32)
    plus2 = jnp.concatenate([plus, plus], 1)
    low2 = jnp.concatenate([lane, lane], 1) < HALF

    def swap(x):
        return pltpu.roll(x, HALF, 1)

    def swap2(x):
        return jnp.concatenate([swap(x[:, :LANES]), swap(x[:, LANES:])], 1)

    for load in loads[:3]:
        load.wait()
    square = (NKD, NKD)
    on = lax.broadcasted_iota(jnp.int32, square, 0) == lax.broadcasted_iota(jnp.int32, square, 1)
    counts = jnp.sum(jnp.where(on, counts_ref[...].astype(jnp.float32), 0.0), axis=1, keepdims=True)
    band = lax.broadcasted_iota(jnp.int32, (NKD, 3 * LANES), 1).astype(jnp.float32)
    weights = jnp.where(band < counts, occ_ref[...], 0.0)
    for k in range(NKD):
        for c in range(2):
            wide[c * KP + k : c * KP + k + 1, :] = row[k, c, 0:1, :].astype(jnp.float32)
    parts = [wide[c * KP : c * KP + NKD, :] * weights for c in range(2)]
    rest = jnp.where(low, parts[0][:, 256:], swap(parts[1][:, 256:]))
    planes = [parts[0][:, :128], parts[1][:, :128], parts[0][:, 128:256], parts[1][:, 128:256], rest]
    block = jnp.concatenate(planes + [jnp.zeros((RD - PLANES * NKD, LANES), jnp.float32)], 0)
    gath[z0, y0] = block.astype(jnp.bfloat16)

    pl.semaphore_wait(barrier, len(peers))

    def send(src, dst, ssem, rsem, peer):
        return pltpu.make_async_remote_copy(
            src_ref=src, dst_ref=dst, send_sem=ssem, recv_sem=rsem, device_id=peer, device_id_type=MESH
        )

    sent = []

    def go(copy):
        copy.start()
        sent.append(copy)

    def along(o, dz):
        ref, to = gath.at[zz(o), y0], (o - dz) % 16
        return send(ref, ref, sz.at[to], rz.at[to], zdev(dz))

    def chain(o):
        rows, to = (pl.ds(0, CUT), 8) if o > 0 else (pl.ds(CUT, RD - CUT), 16)
        ref = gath.at[zz(o), y0, rows]
        return send(ref, ref, sz.at[to], rz.at[to], zdev(-o))

    def chained(o):
        rows, to = (pl.ds(0, CUT), 8) if o > 0 else (pl.ds(CUT, RD - CUT), 16)
        ref = gath.at[zz(8), y0, rows]
        return send(ref, ref, sz.at[to], rz.at[to], zdev(-o))

    def across(i, o, y):
        ref = gath.at[zz(o), y]
        return send(ref, ref, sy.at[i, o % 16], ry.at[i, o % 16], ydev((1, 3)[i]))

    def onward(o, y):
        ref = gath.at[zz(o), y]
        return send(ref, ref, sf.at[o % 16], rf.at[o % 16], ydev((1, 3)[OFFSETS.index(o) % 2]))

    def near(o):
        for dz in NEAR[o]:
            go(along(o, dz))

    def sides(o):
        for i in range(2):
            go(across(i, o, y0))

    def arrive(o):
        ref = gath.at[zz(o), y0]
        send(ref, ref, sz.at[o % 16], rz.at[o % 16], zdev(1)).wait_recv()
        sides(o)

    def pass_on(o):
        for i in range(2):
            across(i, o, yy((3, 1)[i])).wait_recv()
        go(onward(o, yy((3, 1)[OFFSETS.index(o) % 2])))

    sides(0)
    for dz in (4, -4):
        go(along(0, dz))
    near(0)

    loads[3].wait()
    for k in range(NKD, KP):
        dense[pl.ds(k, 64, stride=KP), :] = jnp.zeros((64, LANES), jnp.float32)

    def lay(k, carry):
        pair = jnp.concatenate([cou[k, 0], cou[k, 1]], axis=1).astype(jnp.float32)
        dense[pl.ds(k, 64, stride=KP), :] = pair
        return carry

    lax.fori_loop(0, NKD, lay, 0, unroll=9)
    vsend[...] = dense[...].astype(jnp.bfloat16).reshape(8, 8, KP, LANES)

    def move(stage, src, dst, d):
        return send(src, dst, sx.at[stage, d - 1], rx.at[stage, d - 1], adev(d))

    def theirs(d):
        return lax.rem(a0 + 8 - d, 8)

    for d in range(1, 8):
        go(move(0, vsend.at[lax.rem(a0 + d, 8)], vrecv.at[:, a0], d))
    vrecv[:, a0] = vsend[a0]

    def turn(k, carry):
        re, im = orb[k, 0], orb[k, 1]
        minus = -im
        rest_re = jnp.where(low, re[:, 256:].astype(jnp.float32), swap(im[:, 256:].astype(jnp.float32)))
        rest_im = jnp.where(low, minus[:, 256:].astype(jnp.float32), swap(re[:, 256:].astype(jnp.float32)))
        right[k, 0:64, :] = jnp.concatenate(
            [re[:, :128], im[:, :128], re[:, 128:256], im[:, 128:256], rest_re.astype(jnp.bfloat16)], 1
        )
        right[k, 64:128, :] = jnp.concatenate(
            [minus[:, :128], re[:, :128], minus[:, 128:256], re[:, 128:256], rest_im.astype(jnp.bfloat16)], 1
        )
        return carry

    def scatter(stage, start, count):
        first_group, groups = STAGES[stage]
        base, rows = first_group * 16 * RD, groups * 16

        def one(i, carry):
            z = lax.rem(z0 + start + i, 16)
            for u in range(groups):
                y = yy(DELTA_Y[first_group + u])
                spread[pl.ds(base + u * 16 + z, RD, stride=rows), :] = gath[z, y].astype(jnp.float32)
            return carry

        lax.fori_loop(0, count, one, 0)

    def dens(stage, start, stop):
        first_group, groups = STAGES[stage]
        base, rows = first_group * 16 * RD, groups * 16

        def one(k, carry):
            left = [
                spread[pl.ds(pl.multiple_of(base + (j * NKD + k) * rows, 16), rows), :].astype(jnp.bfloat16)
                for j in range(PLANES)
            ]
            d = lax.dot_general(
                jnp.concatenate(left, 1), right[k], (((1,), (1,)), ((), ())), preferred_element_type=jnp.float32
            )
            dense[pl.ds(first_group * 16 * KP + k, rows, stride=KP), :] = d
            return carry

        lax.fori_loop(start, stop, one, 0, unroll=27)

    def hand_over(stage):
        first_group, groups = STAGES[stage]
        for u in range(first_group, first_group + groups):
            d = dense[u * 16 * KP : (u + 1) * 16 * KP, :].astype(jnp.bfloat16)
            dsend[:, 2 * u : 2 * u + 2] = d.reshape(8, 2, KP, LANES)
        part = pl.ds(2 * first_group, 2 * groups)
        for d in range(1, 8):
            go(move(1 + stage, dsend.at[lax.rem(a0 + d, 8), part], drecv.at[part, a0], d))
        drecv[part, a0] = dsend[a0, part]

    def forward(x):
        y = jnp.dot(table_ref[...], x, preferred_element_type=jnp.float32)
        return y[:PTILE] + (ROOT * plus2) * swap2(y[PTILE:])

    def pair(ref, i, j):
        return jnp.concatenate([ref[i].reshape(PTILE, LANES), ref[j].reshape(PTILE, LANES)], 1)

    def convolve(stage):
        first_group, groups = STAGES[stage]
        part = pl.ds(2 * first_group, 2 * groups)
        for d in range(1, 8):
            move(1 + stage, dsend.at[0, part], drecv.at[part, theirs(d)], d).wait_recv()
        for u in range(first_group, first_group + groups):
            d = forward(pair(drecv, 2 * u, 2 * u + 1))
            y = yy(DELTA_Y[u])
            product = vhat_a[y] * d + vhat_b[y] * swap2(d)
            t = jnp.dot(table_ref[...], product.astype(jnp.bfloat16), preferred_element_type=jnp.float32)
            back = SCALE * t[:PTILE] - (SCALE * ROOT * plus2) * swap2(t[PTILE:])
            back = back.astype(jnp.bfloat16)
            osend[2 * u] = back[:, :LANES].reshape(8, KP, LANES)
            osend[2 * u + 1] = back[:, LANES:].reshape(8, KP, LANES)
        for d in range(1, 8):
            go(move(4 + stage, osend.at[part, lax.rem(a0 + d, 8)], orecv.at[a0, part], d))
        orecv[a0, part] = osend[part, a0]

    def unlay(stage):
        first_group, groups = STAGES[stage]
        part = pl.ds(2 * first_group, 2 * groups)
        for d in range(1, 8):
            move(4 + stage, osend.at[part, 0], orecv.at[theirs(d), part], d).wait_recv()

        def one(a, carry):
            for u in range(first_group, first_group + groups):
                for i in range(2):
                    r = (2 * a + i) * 4 + yy(DELTA_Y[u])
                    spread[pl.ds(r, KP, stride=64), :] = orecv[a, 2 * u + i].astype(jnp.float32)
            return carry

        lax.fori_loop(0, 8, one, 0, unroll=4)

    for o in (-1, 1, -2, 2):
        arrive(o)
    pass_on(0)
    for o in (-4, 4):
        arrive(o)
        go(chain(o))
        near(o)
    loads[4].wait()
    lax.fori_loop(0, 9, turn, 0, unroll=9)
    for o in (-5, 3, -3, 5, -6, 6):
        arrive(o)
    for o in (-1, 1, -2, 2):
        pass_on(o)
    for o in (4, -4):
        chained(o).wait_recv()
    sides(8)
    near(8)
    lax.fori_loop(9, 18, turn, 0, unroll=9)
    for o in (-4, 4):
        pass_on(o)
    for o in (7, -7):
        arrive(o)
    lax.fori_loop(18, NKD, turn, 0, unroll=9)
    scatter(0, 10, 7)
    for o in (-5, 3, -3):
        pass_on(o)
    scatter(0, 1, 9)
    for o in (5, -6, 6):
        pass_on(o)
    for k in range(NKD, KP):
        dense[pl.ds(k, 64, stride=KP), :] = jnp.zeros((64, LANES), jnp.float32)
    dens(0, 0, NKD)
    hand_over(0)
    for o in (8, 7, -7):
        pass_on(o)

    loads[5].wait()
    for d in range(1, 8):
        move(0, vsend.at[0], vrecv.at[:, theirs(d)], d).wait_recv()

    def kern(y):
        v = forward(pair(vrecv, y, y + 4))
        w = swap2(v)
        vhat_a[y] = jnp.where(low2, v, w)
        vhat_b[y] = jnp.where(low2, -w, v)

    for y in range(4):
        kern(y)
    scatter(1, 0, 16)
    dens(1, 0, NKD)
    hand_over(1)
    convolve(0)
    for o in OFFSETS[:13]:
        onward(o, yy(2)).wait_recv()
    scatter(2, 10, 13)
    for o in OFFSETS[13:]:
        onward(o, yy(2)).wait_recv()
    scatter(2, 7, 3)
    dens(2, 0, NKD)
    hand_over(2)
    convolve(1)
    unlay(0)
    convolve(2)
    unlay(1)
    unlay(2)

    def finish(k, carry):
        o = spread[pl.ds(pl.multiple_of(k * 64, 64), 64), :]
        out_ref[k, 0] = o[:, :HALF].astype(jnp.bfloat16)
        out_ref[k, 1] = swap(o)[:, :HALF].astype(jnp.bfloat16)
        return carry

    lax.fori_loop(0, NKD, finish, 0, unroll=9)
    for copy in sent:
        copy.wait_send()


def local(orbitals, counts, occupation, coulomb):
    table = jnp.asarray(transform_table(), jnp.bfloat16)
    bf, f32 = jnp.bfloat16, jnp.float32
    vmem = pltpu.VMEM
    dma = pltpu.SemaphoreType.DMA
    return pl.pallas_call(
        kernel,
        out_shape=jax.ShapeDtypeStruct((NKD, 2, 64, 64), bf),
        in_specs=[pl.BlockSpec(memory_space=pltpu.HBM)] * 5,
        out_specs=pl.BlockSpec(memory_space=vmem),
        scratch_shapes=[
            vmem((NKD, 2, 16, 384), bf),
            vmem((1, NKD), jnp.int32),
            vmem((NKD, 384), f32),
            vmem((NKD, 2, 64, 384), bf),
            vmem((NKD, 2, 64, 64), bf),
            vmem((2 * PTILE, PTILE), bf),
            vmem((NKD, 128, PLANES * LANES), bf),
            vmem((16, 4, RD, LANES), bf),
            vmem((RD * 64, LANES), f32),
            vmem((2 * KP, 384), f32),
            vmem((64 * KP, LANES), f32),
            vmem((8, 8, KP, LANES), bf),
            vmem((8, 8, KP, LANES), bf),
            vmem((4, PTILE, 2 * LANES), f32),
            vmem((4, PTILE, 2 * LANES), f32),
            vmem((8, 8, KP, LANES), bf),
            vmem((8, 8, KP, LANES), bf),
            vmem((8, 8, KP, LANES), bf),
            vmem((8, 8, KP, LANES), bf),
            dma((6,)),
            dma((17,)),
            dma((17,)),
            dma((2, 16)),
            dma((2, 16)),
            dma((16,)),
            dma((16,)),
            dma((7, 7)),
            dma((7, 7)),
        ],
        compiler_params=pltpu.CompilerParams(
            collective_id=0, has_side_effects=True, vmem_limit_bytes=60 * 1024 * 1024
        ),
    )(orbitals, counts.reshape(1, NKD), occupation, coulomb, table)


def solution(mesh):
    finer = Mesh(mesh.devices.reshape(4, 2, 16, 4), ("ka_0", "ka_1", "pts_0", "pts_1"))
    in_specs = (P(KA, None, PTS, None), P(KA), P(KA, None), P(KA, None, None, PTS))
    out_specs = P(KA, None, None, PTS)
    return jax.shard_map(local, mesh=finer, in_specs=in_specs, out_specs=out_specs, check_vma=False)
```
